32 devices in a mesh: group: 2 (over x), dp: 8 (over z, y), adapter: 2 (over core).
Axes of the slice: x: 2, y: 2, z: 4, core: 2. Of those that a mesh axis runs over, the one named last changes fastest.
Arguments:
- hidden_input: bfloat16 [16384, 4096], P(('group', 'dp', 'adapter')), parts along dimension 0, may hold values from -6 to 6
- output_gradient: bfloat16 [16384, 1024], P(('group', 'dp', 'adapter')), parts along dimension 0, may hold values from -0.25 to 0.25
- frozen_value_weight: bfloat16 [4096, 1024], P('dp'), may hold values from -0.09375 to 0.09375
- adapter_down_maps: bfloat16 [64, 16, 4096], P('group', None, ('dp', 'adapter')), parts along dimension 0, may hold values from -0.09375 to 0.09375
- adapter_up_maps: bfloat16 [64, 16, 1024], P('group', None, ('dp', 'adapter')), parts along dimension 0, may hold values from -1.5 to 1.5
- segment_length_quota: int32 [32, 8], P(('group', 'dp', 'adapter')), parts along dimension 0, may hold values from 1 to 256, 512 in all within a row
- segment_tenant_id: int32 [32, 8], P(('group', 'dp', 'adapter')), parts along dimension 0, may hold values from 0 to 31
- tenant_adapter_slot: int32 [64], P('group'), parts along dimension 0, may hold values from 0 to 31, each once
Outputs:
- input_gradient: bfloat16 [16384, 4096], P(('group', 'dp', 'adapter')), parts along dimension 0
- down_map_gradient: float32 [64, 16, 4096], P('group', None, ('dp', 'adapter')), parts along dimension 0
- up_map_gradient: float32 [64, 16, 1024], P('group', None, ('dp', 'adapter')), parts along dimension 0
The draws below stay inside these ranges and needn't reach their ends.
There are 2 independent parts, one for each index of `group`. The reference program is written for one: setup_inputs(seed, part) draws one part's arguments, and reference() takes and returns one part's arrays. A program takes and returns all parts, laid end to end along the dimension named above; an argument that names none is the same for every part. Nothing has to cross between parts.
Inputs may be any that keep to these rules, and one draw needn't show every extreme that they name: `segment_length_quota`: each row's quotas sum to 512; some segment of each row has exactly 256 tokens. `tenant_adapter_slot`: A permutation of the slots.
All inputs are finite; a program needn't handle non-finite values.
Results may differ from the reference program's by a relative error of at most 0.0046.
Values may be sent and summed in bfloat16 or wider, within the bound.
A program may use at most 256 MiB of HBM per device.

```python
import math
import jax
import jax.numpy as jnp
import numpy as np
from jax import lax

MODEL_WIDTH = 4096
VALUE_OUTPUTS = 1024
ADAPTER_RANK = 16
SEG = 8
TOK_DEV = 512
TENANT_ADAPTERS = 32
ROWS = 16
TOKENS = 8192


def place_ends(result, rng, low, top_value):
    spot = [jax.random.randint(jax.random.fold_in(rng, axis), (), 0, length) for axis, length in enumerate(result.shape)]
    longest = result.shape.index(max(result.shape))
    beside = spot[:longest] + [(spot[longest] + 1) % result.shape[longest]] + spot[longest + 1:]
    return result.at[tuple(spot)].set(low).at[tuple(beside)].set(top_value)


def shard_levels(rng, shape, pieces, low, largest):
    def one(dim, blocks):
        draws = jax.random.uniform(jax.random.fold_in(jax.random.fold_in(rng, 6), dim), (blocks,), jnp.float32, low / len(pieces), largest / len(pieces))
        return jnp.repeat(jnp.exp(draws), shape[dim] // blocks).reshape((-1,) + (1,) * (len(shape) - dim - 1))

    loudness = one(*pieces[0])
    for cut in pieces[1:]:
        loudness = loudness * one(*cut)
    return loudness


def length_profile(count, total, reach, lean):
    weights = [(1 << 20) // math.isqrt(grade ** lean) + 1 for grade in range(2, count + 1)]
    rest, holding = total - reach - (count - 1), [1] * (count - 1)
    while rest > 0:
        candidates = [i for i in range(count - 1) if holding[i] < reach]
        whole, remaining = sum([weights[i] for i in candidates]), rest
        for i in candidates:
            extra = min(reach - holding[i], max(1, remaining * weights[i] // whole), rest)
            holding[i] = holding[i] + extra
            rest = rest - extra
    return np.array([reach] + holding)


def uneven(stream_key, count, total, reach, skew):
    if count == 2:
        one = jax.random.randint(stream_key, (), max(1, total - reach), min(reach, total - 1) + 1)
        return jnp.stack([one, total - one])
    sizes = jnp.asarray(length_profile(count, total, reach, skew), jnp.int32)
    pairs = (count - 1) // 2
    giver, receiver = sizes[1:1 + 2 * pairs:2], sizes[2:2 + 2 * pairs:2]
    margin = jnp.minimum(giver - 1, reach - receiver)
    moved = jax.random.randint(jax.random.fold_in(stream_key, 1), (pairs,), 0, 1 << 20) % (margin + 1)
    sizes = sizes.at[1:1 + 2 * pairs:2].set(giver - moved).at[2:2 + 2 * pairs:2].set(receiver + moved)
    return sizes[jax.random.permutation(jax.random.fold_in(stream_key, 2), count)]


def centred(own_key, extent, width, most, shards=(), kind=jnp.bfloat16):
    values = width * jax.random.normal(own_key, extent, jnp.float32)
    if shards:
        values = values * shard_levels(own_key, extent, shards, -0.22, 0.18)
    return jnp.clip(values, -most, most).astype(kind)


def setup_inputs(seed: int = 0, part: int = 0) -> dict:
    seeds = jax.random.split(jax.random.key(seed), 9)
    own_keys = jax.random.split(jax.random.fold_in(seeds[8], part), 9)
    hidden_input = centred(own_keys[0], (TOKENS, MODEL_WIDTH), 1.0, 6.0, ((0, 16),))
    output_gradient = jnp.clip(jax.random.uniform(own_keys[1], (TOKENS, VALUE_OUTPUTS), jnp.float32, -0.25, 0.25) * shard_levels(own_keys[1], (TOKENS, VALUE_OUTPUTS), ((0, 16),), -0.4, 0.0), -0.25, 0.25).astype(jnp.bfloat16)
    frozen_value_weight = centred(seeds[2], (MODEL_WIDTH, VALUE_OUTPUTS), MODEL_WIDTH ** -0.5, 0.09375, ((0, 8),))
    adapter_down_maps = centred(own_keys[3], (TENANT_ADAPTERS, ADAPTER_RANK, MODEL_WIDTH), MODEL_WIDTH ** -0.5, 0.09375, ((2, 16),))
    adapter_up_maps = centred(own_keys[4], (TENANT_ADAPTERS, ADAPTER_RANK, VALUE_OUTPUTS), ADAPTER_RANK ** -0.5, 1.5, ((2, 16),))
    segment_length_quota = jax.vmap(lambda own: uneven(own, SEG, TOK_DEV, TOK_DEV // 2, 2))(jax.random.split(own_keys[5], ROWS)).reshape((ROWS, SEG)).astype(jnp.int32)
    segment_tenant_id = place_ends(jax.random.randint(own_keys[6], (ROWS, SEG), 0, TENANT_ADAPTERS), jax.random.fold_in(own_keys[6], 1), 0, TENANT_ADAPTERS - 1).astype(jnp.int32)
    tenant_adapter_slot = jax.random.permutation(own_keys[7], TENANT_ADAPTERS).astype(jnp.int32)
    return {"hidden_input": hidden_input, "output_gradient": output_gradient, "frozen_value_weight": frozen_value_weight, "adapter_down_maps": adapter_down_maps, "adapter_up_maps": adapter_up_maps, "segment_length_quota": segment_length_quota, "segment_tenant_id": segment_tenant_id, "tenant_adapter_slot": tenant_adapter_slot}


adapter_scale = 2.0


def token_slots(segment_length_quota, segment_tenant_id, tenant_adapter_slot, tok):
    segs = segment_length_quota.shape[1]
    bounds = jnp.cumsum(segment_length_quota, axis=1).astype(jnp.int32)
    position = lax.iota(jnp.int32, tok)
    inside = (position[None, :, None] >= bounds[:, None, :]).astype(jnp.int32)
    seg_index = jnp.sum(inside, axis=2)
    seg_hot = (seg_index[:, :, None] == lax.iota(jnp.int32, segs)[None, None, :]).astype(jnp.int32)
    tenant = jnp.sum(seg_hot * segment_tenant_id[:, None, :], axis=2)
    segment_count = tenant_adapter_slot.shape[0]
    tenant_hot = (tenant[:, :, None] == lax.iota(jnp.int32, segment_count)[None, None, :]).astype(jnp.int32)
    slot = jnp.sum(tenant_hot * tenant_adapter_slot[None, None, :], axis=2)
    return seg_hot, slot


def reference(hidden_input, output_gradient, frozen_value_weight, adapter_down_maps, adapter_up_maps, segment_length_quota, segment_tenant_id, tenant_adapter_slot):
    segment_count, adapter_rank_size, feature_width = adapter_down_maps.shape
    seg_hot, slot = token_slots(segment_length_quota, segment_tenant_id, tenant_adapter_slot, TOK_DEV)
    slot = slot.reshape(-1)
    slot_hot = (slot[:, None] == lax.iota(jnp.int32, segment_count)[None, :]).astype(jnp.float32)
    segment_mask_table = jnp.repeat(slot_hot, adapter_rank_size, axis=1)
    down_flattened = adapter_down_maps.reshape(segment_count * adapter_rank_size, feature_width)
    up_flattened = adapter_up_maps.reshape(segment_count * adapter_rank_size, adapter_up_maps.shape[2])
    adapter_input = (jnp.dot(hidden_input, down_flattened.T, preferred_element_type=jnp.float32) * segment_mask_table).astype(jnp.bfloat16)
    adapter_gradient = (adapter_scale * jnp.dot(output_gradient, up_flattened.T, preferred_element_type=jnp.float32) * segment_mask_table).astype(jnp.bfloat16)
    base_product = jnp.dot(output_gradient, frozen_value_weight.T, preferred_element_type=jnp.float32)
    input_gradient = (base_product + jnp.dot(adapter_gradient, down_flattened, preferred_element_type=jnp.float32)).astype(jnp.bfloat16)
    down_map_gradient = jnp.dot(adapter_gradient.T, hidden_input, preferred_element_type=jnp.float32).reshape(segment_count, adapter_rank_size, feature_width)
    up_map_gradient = adapter_scale * jnp.dot(adapter_input.T, output_gradient, preferred_element_type=jnp.float32)
    return input_gradient, down_map_gradient, up_map_gradient.reshape(segment_count, adapter_rank_size, adapter_up_maps.shape[2])
```

```python
import functools

import jax
import jax.numpy as jnp
from jax import lax
from jax.experimental import pallas as pl
from jax.experimental.pallas import tpu as pltpu
from jax.sharding import PartitionSpec as P

adapter_scale = 2.0
MESH = pl.DeviceIdType.MESH


def ring_position(d, n):
    odd = lax.rem(d, 2)
    half = lax.div(d, 2)
    return (1 - odd) * half + odd * (n - 1 - half)


def ring_device(p, n):
    p = lax.rem(p + n, n)
    upper = lax.div(p, n // 2)
    return (1 - upper) * (2 * p) + upper * (2 * (n - 1 - p) + 1)


class Ring:
    def __init__(self, n, items, sems):
        self.n, self.items = n, items
        self.ring_send, self.ring_recv, self.side_send, self.side_recv, self.local = sems
        self.me = lax.axis_index("dp")
        self.lane = lax.axis_index("adapter")
        self.pos = ring_position(self.me, n)
        self.right = ring_device(self.pos + 1, n)
        self.left = ring_device(self.pos + n - 1, n)
        self.steps = n // 2
        self.copies = {}
        self.sides = []
        self.locals = []

    def window(self, item, device, step, way):
        rows = item[2]
        if step < self.steps - 1:
            return 0, rows
        if rows % 32 == 0:
            return (0, rows // 2) if way == 0 else (rows // 2, rows // 2)
        return (0, rows) if way == 0 else (0, 0)

    def target_rows(self, item, device, lane, start, count):
        rows = item[2]
        return item[1].at[pl.ds(pl.multiple_of((device * 2 + lane) * rows + start, 16), count)]

    def begin(self):
        for i, item in enumerate(self.items):
            source, target, rows, shared = item
            if shared:
                own = pltpu.make_async_copy(
                    source, target.at[pl.ds(pl.multiple_of(self.me * 2 * rows, 16), 2 * rows)], self.local.at[i]
                )
            else:
                own = pltpu.make_async_copy(
                    source, self.target_rows(item, self.me, self.lane, 0, rows), self.local.at[i]
                )
            own.start()
            self.locals.append(own)
        for i in range(len(self.items)):
            self.send(i, 0)
        for i, item in enumerate(self.items):
            if not item[3]:
                self.side(i, item[0], self.me, 0, item[2], 0)

    def send(self, i, step):
        item = self.items[i]
        for way in (0, 1):
            start, count = self.window(item, None, step, way)
            if count == 0:
                continue
            back = self.n - step if way == 0 else step
            device = ring_device(self.pos + back, self.n)
            target = self.target_rows(item, device, self.lane, start, count)
            if step == 0:
                base = pl.multiple_of(self.lane * item[2] + start, 16) if item[3] else start
                source = item[0].at[pl.ds(base, count)]
            else:
                source = target
            copy = pltpu.make_async_remote_copy(
                src_ref=source,
                dst_ref=target,
                send_sem=self.ring_send.at[i, way, step],
                recv_sem=self.ring_recv.at[i, way, step],
                device_id={"dp": self.right if way == 0 else self.left},
                device_id_type=MESH,
            )
            copy.start()
            self.copies[i, way, step] = copy

    def side(self, i, source, device, start, count, slot):
        item = self.items[i]
        copy = pltpu.make_async_remote_copy(
            src_ref=source,
            dst_ref=self.target_rows(item, device, self.lane, start, count),
            send_sem=self.side_send.at[i, slot],
            recv_sem=self.side_recv.at[i, slot],
            device_id={"adapter": 1 - self.lane},
            device_id_type=MESH,
        )
        copy.start()
        self.sides.append(copy)

    def run(self):
        for step in range(self.steps):
            for i, item in enumerate(self.items):
                for way in (0, 1):
                    if (i, way, step) in self.copies:
                        self.copies[i, way, step].wait_recv()
                if step + 1 < self.steps:
                    self.send(i, step + 1)
                for way in (0, 1):
                    start, count = self.window(item, None, step, way)
                    if count == 0:
                        continue
                    ahead = self.n - 1 - step if way == 0 else 1 + step
                    device = ring_device(self.pos + ahead, self.n)
                    block = self.target_rows(item, device, self.lane, start, count)
                    self.side(i, block, device, start, count, 1 + 2 * step + way)

    def finish(self):
        for copy in self.copies.values():
            copy.wait_send()
        for copy in self.sides:
            copy.wait()
        for copy in self.locals:
            copy.wait()


def ring_scratch(n, items):
    return [
        pltpu.SemaphoreType.DMA((items, 2, n // 2)),
        pltpu.SemaphoreType.DMA((items, 2, n // 2)),
        pltpu.SemaphoreType.DMA((items, 1 + n)),
        pltpu.SemaphoreType.DMA((items, 1 + n)),
        pltpu.SemaphoreType.DMA((items,)),
    ]


def greet_ring(barrier, n):
    lane, pos = lax.axis_index("adapter"), ring_position(lax.axis_index("dp"), n)
    for device in (ring_device(pos + 1, n), ring_device(pos + n - 1, n)):
        pl.semaphore_signal(barrier, inc=1, device_id={"dp": device}, device_id_type=MESH)
    pl.semaphore_signal(barrier, inc=1, device_id={"adapter": 1 - lane}, device_id_type=MESH)
    pl.semaphore_wait(barrier, 3)


def maps_kernel(n, down_ref, up_ref, down_out, up_out, *sems):
    greet_ring(pltpu.get_barrier_semaphore(), n)
    ring = Ring(n, [(down_ref, down_out, down_ref.shape[0], False), (up_ref, up_out, up_ref.shape[0], False)], sems)
    ring.begin()
    ring.run()
    ring.finish()


def weight_kernel(n, weight_ref, down_ref, up_ref, hot_ref, weight_out, down_out, up_out, hot_out, *sems):
    devices = 2 * n
    ring_sems, (send_sem, recv_sem, local_sem) = sems[:5], sems[5:]
    me = lax.axis_index("dp") * 2 + lax.axis_index("adapter")
    barrier = pltpu.get_barrier_semaphore()

    def peer_of(k):
        peer = lax.rem(me + k, devices)
        return {"dp": lax.div(peer, 2), "adapter": lax.rem(peer, 2)}, peer

    def greet(k, carry):
        pl.semaphore_signal(barrier, inc=1, device_id=peer_of(k)[0], device_id_type=MESH)
        return carry

    lax.fori_loop(1, devices, greet, 0)
    pl.semaphore_wait(barrier, devices - 1)

    rows_down, rows_up = down_out.shape[0], up_out.shape[0]
    wide = down_ref.shape[1]

    def parts(owner, sender):
        place = pl.ds(pl.multiple_of(sender * wide, 128), wide)
        return (
            (down_ref.at[pl.ds(pl.multiple_of(owner * rows_down, 16), rows_down)], down_out.at[:, place]),
            (up_ref.at[pl.ds(pl.multiple_of(owner * rows_up, 16), rows_up)], up_out.at[:, place]),
            (hot_ref, hot_out.at[sender]),
        )

    def copies(k):
        device, peer = peer_of(k)
        return [
            pltpu.make_async_remote_copy(
                src_ref=source,
                dst_ref=target,
                send_sem=send_sem.at[i, k],
                recv_sem=recv_sem.at[i, k],
                device_id=device,
                device_id_type=MESH,
            )
            for i, (source, target) in enumerate(parts(peer, me))
        ]

    ring = Ring(n, [(weight_ref, weight_out, weight_ref.shape[0] // 2, True)], ring_sems)

    def start(k, carry):
        for copy in copies(k):
            copy.start()
        return carry

    own = [
        pltpu.make_async_copy(source, target, local_sem.at[i]) for i, (source, target) in enumerate(parts(me, me))
    ]
    for copy in own:
        copy.start()
    ring.begin()
    lax.fori_loop(1, devices, start, 0)
    ring.run()
    ring.finish()

    def end(k, carry):
        for copy in copies(k):
            copy.wait()
        return carry

    lax.fori_loop(1, devices, end, 0)
    for copy in own:
        copy.wait()


def call(kernel, outs, operands, scratch, collective_id):
    anywhere = pl.BlockSpec(memory_space=pl.ANY)
    return pl.pallas_call(
        kernel,
        out_shape=outs,
        in_specs=[anywhere] * len(operands),
        out_specs=[anywhere] * len(outs),
        scratch_shapes=scratch,
        compiler_params=pltpu.CompilerParams(collective_id=collective_id, has_side_effects=True),
    )(*operands)


def token_slots(segment_length_quota, segment_tenant_id, tenant_adapter_slot, tok):
    ends = jnp.cumsum(segment_length_quota[0])
    starts = ends - segment_length_quota[0]
    position = lax.iota(jnp.int32, tok)[:, None]
    seg_hot = (position >= starts[None, :]) & (position < ends[None, :])
    count = tenant_adapter_slot.shape[0]
    tenant_hot = segment_tenant_id[0][:, None] == lax.iota(jnp.int32, count)[None, :]
    slot = jnp.sum(tenant_hot.astype(jnp.int32) * tenant_adapter_slot[None, :], axis=1)
    return seg_hot, slot


def dot(left, right, left_dim, right_dim):
    return lax.dot_general(
        left, right, (((left_dim,), (right_dim,)), ((), ())), preferred_element_type=jnp.float32
    )


def shards(
    n,
    hidden_input,
    output_gradient,
    frozen_value_weight,
    adapter_down_maps,
    adapter_up_maps,
    segment_length_quota,
    segment_tenant_id,
    tenant_adapter_slot,
):
    tok, width = hidden_input.shape
    outputs = output_gradient.shape[1]
    slots, rank, down_columns = adapter_down_maps.shape
    up_columns = adapter_up_maps.shape[2]
    segs = segment_length_quota.shape[1]
    flat, wide, devices = slots * rank, segs * rank, 2 * n
    bf16 = jnp.bfloat16

    down_own = adapter_down_maps.reshape(flat, down_columns).T
    up_own = adapter_up_maps.reshape(flat, up_columns).T
    down, up = call(
        functools.partial(maps_kernel, n),
        [jax.ShapeDtypeStruct((width, flat), bf16), jax.ShapeDtypeStruct((outputs, flat), bf16)],
        [down_own, up_own],
        ring_scratch(n, 2),
        0,
    )

    seg_hot, slot = token_slots(segment_length_quota, segment_tenant_id, tenant_adapter_slot, tok)
    slot_hot = slot[:, None] == lax.iota(jnp.int32, slots)[None, :]
    seg_mask = jnp.repeat(seg_hot.astype(jnp.float32), rank, axis=1)
    token_hot = dot(seg_hot.astype(bf16), slot_hot.astype(bf16), 1, 0)
    mask = jnp.repeat(token_hot, rank, axis=1)
    fold = (
        lax.rem(lax.iota(jnp.int32, flat), rank)[:, None] == lax.rem(lax.iota(jnp.int32, wide), rank)[None, :]
    ).astype(bf16)

    lora_in = (dot(hidden_input, down, 1, 0) * mask).astype(bf16)
    lora_grad = (adapter_scale * dot(output_gradient, up, 1, 0) * mask).astype(bf16)
    lora_in_seg = (dot(lora_in, fold, 1, 0) * seg_mask).astype(bf16)
    lora_grad_seg = (dot(lora_grad, fold, 1, 0) * seg_mask).astype(bf16)
    down_term = dot(hidden_input, lora_grad_seg, 0, 0).astype(bf16)
    up_term = (adapter_scale * dot(output_gradient, lora_in_seg, 0, 0)).astype(bf16)

    hot = jnp.pad(slot_hot.astype(bf16), ((0, 16 - segs % 16), (0, 128 - slots % 128)))
    weight, down_parts, up_parts, hots = call(
        functools.partial(weight_kernel, n),
        [
            jax.ShapeDtypeStruct((width, outputs), bf16),
            jax.ShapeDtypeStruct((down_columns, devices * wide), bf16),
            jax.ShapeDtypeStruct((up_columns, devices * wide), bf16),
            jax.ShapeDtypeStruct((devices,) + hot.shape, bf16),
        ],
        [frozen_value_weight, down_term, up_term, hot],
        ring_scratch(n, 1)
        + [pltpu.SemaphoreType.DMA((3, devices)), pltpu.SemaphoreType.DMA((3, devices)), pltpu.SemaphoreType.DMA((3,))],
        1,
    )

    spread = jnp.repeat(jnp.repeat(hots[:, :segs, :slots].reshape(devices * segs, slots), rank, axis=0), rank, axis=1)
    same_rank = (
        lax.rem(lax.iota(jnp.int32, devices * wide), rank)[:, None]
        == lax.rem(lax.iota(jnp.int32, flat), rank)[None, :]
    )
    spread = jnp.where(same_rank, spread, jnp.zeros_like(spread))
    down_map_gradient = dot(spread, down_parts, 0, 1).reshape(slots, rank, down_columns)
    up_map_gradient = dot(spread, up_parts, 0, 1).reshape(slots, rank, up_columns)

    input_gradient = (dot(output_gradient, weight, 1, 1) + dot(lora_grad, down, 1, 1)).astype(bf16)
    return (input_gradient, down_map_gradient, up_map_gradient)


def solution(mesh):
    return jax.shard_map(
        functools.partial(shards, mesh.shape["dp"]),
        mesh=mesh,
        in_specs=(
            P(("group", "dp", "adapter"), None),
            P(("group", "dp", "adapter"), None),
            P("dp", None),
            P("group", None, ("dp", "adapter")),
            P("group", None, ("dp", "adapter")),
            P(("group", "dp", "adapter"), None),
            P(("group", "dp", "adapter"), None),
            P("group"),
        ),
        out_specs=(
            P(("group", "dp", "adapter"), None),
            P("group", None, ("dp", "adapter")),
            P("group", None, ("dp", "adapter")),
        ),
        check_vma=False,
    )
```

```python
import functools

import jax
import jax.numpy as jnp
from jax import lax
from jax.experimental import pallas as pl
from jax.experimental.pallas import tpu as pltpu
from jax.sharding import PartitionSpec as P

adapter_scale = 2.0
MESH = pl.DeviceIdType.MESH


def ring_position(d, n):
    odd = lax.rem(d, 2)
    half = lax.div(d, 2)
    return (1 - odd) * half + odd * (n - 1 - half)


def ring_device(p, n):
    p = lax.rem(p + n, n)
    upper = lax.div(p, n // 2)
    return (1 - upper) * (2 * p) + upper * (2 * (n - 1 - p) + 1)


class Ring:
    def __init__(self, n, items, sems):
        self.n, self.items = n, items
        self.ring_send, self.ring_recv, self.side_send, self.side_recv, self.local = sems[:5]
        self.pair_sems = sems[5:]
        self.me = lax.axis_index("dp")
        self.group = lax.axis_index("group")
        self.half = lax.rem(self.group, 2)
        self.pairs = {}
        self.lane = lax.axis_index("adapter")
        self.pos = ring_position(self.me, n)
        self.right = ring_device(self.pos + 1, n)
        self.left = ring_device(self.pos + n - 1, n)
        self.steps = n // 2
        self.copies = {}
        self.sides = []
        self.locals = []

    def window(self, item, device, step, way):
        rows = item[2]
        if step < self.steps - 1:
            return 0, rows
        if rows % 32 == 0:
            return (0, rows // 2) if way == 0 else (rows // 2, rows // 2)
        return (0, rows) if way == 0 else (0, 0)

    def target_rows(self, item, device, lane, start, count, half=None):
        rows = item[2]
        if item[3]:
            half = self.half if half is None else half
            block = device * 4 + half * 2 + lane
        else:
            block = device * 2 + lane
        return item[1].at[pl.ds(pl.multiple_of(block * rows + start, 16), count)]

    def begin(self):
        for i, item in enumerate(self.items):
            source, target, rows, shared = item
            if shared:
                own = pltpu.make_async_copy(
                    source, target.at[pl.ds(pl.multiple_of(self.me * 4 * rows, 16), 4 * rows)], self.local.at[i]
                )
            else:
                own = pltpu.make_async_copy(
                    source, self.target_rows(item, self.me, self.lane, 0, rows), self.local.at[i]
                )
            own.start()
            self.locals.append(own)
        for i in range(len(self.items)):
            self.send(i, 0)
        for i, item in enumerate(self.items):
            if not item[3]:
                self.side(i, item[0], self.me, 0, item[2], 0)

    def send(self, i, step):
        item = self.items[i]
        for way in (0, 1):
            start, count = self.window(item, None, step, way)
            if count == 0:
                continue
            back = self.n - step if way == 0 else step
            device = ring_device(self.pos + back, self.n)
            target = self.target_rows(item, device, self.lane, start, count)
            if step == 0:
                base = start
                if item[3]:
                    base = pl.multiple_of((self.half * 2 + self.lane) * item[2] + start, 16)
                source = item[0].at[pl.ds(base, count)]
            else:
                source = target
            copy = pltpu.make_async_remote_copy(
                src_ref=source,
                dst_ref=target,
                send_sem=self.ring_send.at[i, way, step],
                recv_sem=self.ring_recv.at[i, way, step],
                device_id={"dp": self.right if way == 0 else self.left},
                device_id_type=MESH,
            )
            copy.start()
            self.copies[i, way, step] = copy

    def pair(self, i, block, slot):
        copy = pltpu.make_async_remote_copy(
            src_ref=block,
            dst_ref=block,
            send_sem=self.pair_sems[0].at[i, slot],
            recv_sem=self.pair_sems[1].at[i, slot],
            device_id={"group": self.group + 1 - 2 * self.half},
            device_id_type=MESH,
        )
        copy.start()
        self.pairs[i, slot] = copy

    def side(self, i, source, device, start, count, slot, half=None):
        item = self.items[i]
        copy = pltpu.make_async_remote_copy(
            src_ref=source,
            dst_ref=self.target_rows(item, device, self.lane, start, count, half),
            send_sem=self.side_send.at[i, slot],
            recv_sem=self.side_recv.at[i, slot],
            device_id={"adapter": 1 - self.lane},
            device_id_type=MESH,
        )
        copy.start()
        self.sides.append(copy)

    def arrived(self, step):
        for i, item in enumerate(self.items):
            for way in (0, 1):
                start, count = self.window(item, None, step, way)
                if count:
                    ahead = self.n - 1 - step if way == 0 else 1 + step
                    yield i, 1 + 2 * step + way, ring_device(self.pos + ahead, self.n), start, count

    def run(self):
        for step in range(self.steps):
            for i, item in enumerate(self.items):
                for way in (0, 1):
                    if (i, way, step) in self.copies:
                        self.copies[i, way, step].wait_recv()
                if step + 1 < self.steps:
                    self.send(i, step + 1)
            for i, slot, device, start, count in self.arrived(step):
                item = self.items[i]
                block = self.target_rows(item, device, self.lane, start, count)
                if item[3]:
                    self.pair(i, block, slot)
                self.side(i, block, device, start, count, slot)
            if step:
                self.cross(step - 1)
        self.cross(self.steps - 1)

    def cross(self, step):
        for i, slot, device, start, count in self.arrived(step):
            item = self.items[i]
            if item[3]:
                self.pairs[i, slot].wait_recv()
                block = self.target_rows(item, device, self.lane, start, count, 1 - self.half)
                self.side(i, block, device, start, count, self.n + slot, 1 - self.half)

    def finish(self):
        for copy in self.copies.values():
            copy.wait_send()
        for copy in self.pairs.values():
            copy.wait_send()
        for copy in self.sides:
            copy.wait()
        for copy in self.locals:
            copy.wait()


def ring_scratch(n, items):
    return [
        pltpu.SemaphoreType.DMA((items, 2, n // 2)),
        pltpu.SemaphoreType.DMA((items, 2, n // 2)),
        pltpu.SemaphoreType.DMA((items, 1 + 2 * n)),
        pltpu.SemaphoreType.DMA((items, 1 + 2 * n)),
        pltpu.SemaphoreType.DMA((items,)),
    ] + [pltpu.SemaphoreType.DMA((items, 1 + n))] * 2


def greet_ring(barrier, n):
    lane, pos = lax.axis_index("adapter"), ring_position(lax.axis_index("dp"), n)
    for device in (ring_device(pos + 1, n), ring_device(pos + n - 1, n)):
        pl.semaphore_signal(barrier, inc=1, device_id={"dp": device}, device_id_type=MESH)
    pl.semaphore_signal(barrier, inc=1, device_id={"adapter": 1 - lane}, device_id_type=MESH)
    pl.semaphore_wait(barrier, 3)


def maps_kernel(n, down_ref, up_ref, down_out, up_out, *sems):
    greet_ring(pltpu.get_barrier_semaphore(), n)
    ring = Ring(n, [(down_ref, down_out, down_ref.shape[0], False), (up_ref, up_out, up_ref.shape[0], False)], sems)
    ring.begin()
    ring.run()
    ring.finish()


def weight_kernel(n, weight_ref, down_ref, up_ref, hot_ref, weight_out, down_out, up_out, hot_out, *sems):
    devices = 2 * n
    ring_sems, (send_sem, recv_sem, local_sem) = sems[:7], sems[7:]
    me = lax.axis_index("dp") * 2 + lax.axis_index("adapter")
    barrier = pltpu.get_barrier_semaphore()

    def peer_of(k):
        peer = lax.rem(me + k, devices)
        return {"dp": lax.div(peer, 2), "adapter": lax.rem(peer, 2)}, peer

    def greet(k, carry):
        pl.semaphore_signal(barrier, inc=1, device_id=peer_of(k)[0], device_id_type=MESH)
        return carry

    lax.fori_loop(1, devices, greet, 0)
    group = lax.axis_index("group")
    other = group + 1 - 2 * lax.rem(group, 2)
    pl.semaphore_signal(barrier, inc=1, device_id={"group": other}, device_id_type=MESH)
    pl.semaphore_wait(barrier, devices)

    rows_down, rows_up = down_out.shape[0], up_out.shape[0]
    wide = down_ref.shape[1]

    def parts(owner, sender):
        place = pl.ds(pl.multiple_of(sender * wide, 128), wide)
        return (
            (down_ref.at[pl.ds(pl.multiple_of(owner * rows_down, 16), rows_down)], down_out.at[:, place]),
            (up_ref.at[pl.ds(pl.multiple_of(owner * rows_up, 16), rows_up)], up_out.at[:, place]),
            (hot_ref, hot_out.at[sender]),
        )

    def copies(k):
        device, peer = peer_of(k)
        return [
            pltpu.make_async_remote_copy(
                src_ref=source,
                dst_ref=target,
                send_sem=send_sem.at[i, k],
                recv_sem=recv_sem.at[i, k],
                device_id=device,
                device_id_type=MESH,
            )
            for i, (source, target) in enumerate(parts(peer, me))
        ]

    ring = Ring(n, [(weight_ref, weight_out, weight_ref.shape[0] // 4, True)], ring_sems)

    def start(k, carry):
        for copy in copies(k):
            copy.start()
        return carry

    own = [
        pltpu.make_async_copy(source, target, local_sem.at[i]) for i, (source, target) in enumerate(parts(me, me))
    ]
    for copy in own:
        copy.start()
    ring.begin()
    lax.fori_loop(1, devices, start, 0)
    ring.run()
    ring.finish()

    def end(k, carry):
        for copy in copies(k):
            copy.wait()
        return carry

    lax.fori_loop(1, devices, end, 0)
    for copy in own:
        copy.wait()


def call(kernel, outs, operands, scratch, collective_id):
    anywhere = pl.BlockSpec(memory_space=pl.ANY)
    return pl.pallas_call(
        kernel,
        out_shape=outs,
        in_specs=[anywhere] * len(operands),
        out_specs=[anywhere] * len(outs),
        scratch_shapes=scratch,
        compiler_params=pltpu.CompilerParams(collective_id=collective_id, has_side_effects=True),
    )(*operands)


def input_gradient_kernel(grad_ref, weight_ref, lora_ref, down_ref, out_ref):
    total = dot(grad_ref[...], weight_ref[...], 1, 1) + dot(lora_ref[...], down_ref[...], 1, 1)
    out_ref[...] = total.astype(out_ref.dtype)


def input_gradients(output_gradient, weight, lora_grad, down):
    tok, outputs = output_gradient.shape
    width, flat = down.shape
    columns = 512
    return pl.pallas_call(
        input_gradient_kernel,
        grid=(width // columns,),
        out_shape=jax.ShapeDtypeStruct((tok, width), output_gradient.dtype),
        in_specs=[
            pl.BlockSpec((tok, outputs), lambda i: (0, 0)),
            pl.BlockSpec((columns, outputs), lambda i: (i, 0)),
            pl.BlockSpec((tok, flat), lambda i: (0, 0)),
            pl.BlockSpec((columns, flat), lambda i: (i, 0)),
        ],
        out_specs=pl.BlockSpec((tok, columns), lambda i: (0, i)),
        compiler_params=pltpu.CompilerParams(vmem_limit_bytes=32 * 1024 * 1024),
        cost_estimate=pl.CostEstimate(
            flops=2 * tok * width * (outputs + flat),
            bytes_accessed=2 * (width * (outputs + flat) + tok * (outputs + flat + width)),
            transcendentals=0,
        ),
    )(output_gradient, weight, lora_grad, down)


def token_slots(segment_length_quota, segment_tenant_id, tenant_adapter_slot, tok):
    ends = jnp.cumsum(segment_length_quota[0])
    starts = ends - segment_length_quota[0]
    position = lax.iota(jnp.int32, tok)[:, None]
    seg_hot = (position >= starts[None, :]) & (position < ends[None, :])
    count = tenant_adapter_slot.shape[0]
    tenant_hot = segment_tenant_id[0][:, None] == lax.iota(jnp.int32, count)[None, :]
    slot = jnp.sum(tenant_hot.astype(jnp.int32) * tenant_adapter_slot[None, :], axis=1)
    return seg_hot, slot


def dot(left, right, left_dim, right_dim):
    return lax.dot_general(
        left, right, (((left_dim,), (right_dim,)), ((), ())), preferred_element_type=jnp.float32
    )


def shards(
    n,
    hidden_input,
    output_gradient,
    frozen_value_weight,
    adapter_down_maps,
    adapter_up_maps,
    segment_length_quota,
    segment_tenant_id,
    tenant_adapter_slot,
):
    tok, width = hidden_input.shape
    outputs = output_gradient.shape[1]
    slots, rank, down_columns = adapter_down_maps.shape
    up_columns = adapter_up_maps.shape[2]
    segs = segment_length_quota.shape[1]
    flat, wide, devices = slots * rank, segs * rank, 2 * n
    bf16 = jnp.bfloat16

    down_own = adapter_down_maps.reshape(flat, down_columns).T
    up_own = adapter_up_maps.reshape(flat, up_columns).T
    down, up = call(
        functools.partial(maps_kernel, n),
        [jax.ShapeDtypeStruct((width, flat), bf16), jax.ShapeDtypeStruct((outputs, flat), bf16)],
        [down_own, up_own],
        ring_scratch(n, 2),
        0,
    )

    seg_hot, slot = token_slots(segment_length_quota, segment_tenant_id, tenant_adapter_slot, tok)
    slot_hot = slot[:, None] == lax.iota(jnp.int32, slots)[None, :]
    seg_mask = jnp.repeat(seg_hot.astype(jnp.float32), rank, axis=1)
    token_hot = dot(seg_hot.astype(bf16), slot_hot.astype(bf16), 1, 0)
    mask = jnp.repeat(token_hot, rank, axis=1)
    fold = (
        lax.rem(lax.iota(jnp.int32, flat), rank)[:, None] == lax.rem(lax.iota(jnp.int32, wide), rank)[None, :]
    ).astype(bf16)

    lora_in = (dot(hidden_input, down, 1, 0) * mask).astype(bf16)
    lora_grad = (adapter_scale * dot(output_gradient, up, 1, 0) * mask).astype(bf16)
    lora_in_seg = (dot(lora_in, fold, 1, 0) * seg_mask).astype(bf16)
    lora_grad_seg = (dot(lora_grad, fold, 1, 0) * seg_mask).astype(bf16)
    down_term = dot(hidden_input, lora_grad_seg, 0, 0).astype(bf16)
    up_term = (adapter_scale * dot(output_gradient, lora_in_seg, 0, 0)).astype(bf16)

    hot = jnp.pad(slot_hot.astype(bf16), ((0, 16 - segs % 16), (0, 128 - slots % 128)))
    weight, down_parts, up_parts, hots = call(
        functools.partial(weight_kernel, n),
        [
            jax.ShapeDtypeStruct((width, outputs), bf16),
            jax.ShapeDtypeStruct((down_columns, devices * wide), bf16),
            jax.ShapeDtypeStruct((up_columns, devices * wide), bf16),
            jax.ShapeDtypeStruct((devices,) + hot.shape, bf16),
        ],
        [frozen_value_weight, down_term, up_term, hot],
        ring_scratch(n, 1)
        + [pltpu.SemaphoreType.DMA((3, devices)), pltpu.SemaphoreType.DMA((3, devices)), pltpu.SemaphoreType.DMA((3,))],
        1,
    )

    spread = jnp.repeat(jnp.repeat(hots[:, :segs, :slots].reshape(devices * segs, slots), rank, axis=0), rank, axis=1)
    same_rank = (
        lax.rem(lax.iota(jnp.int32, devices * wide), rank)[:, None]
        == lax.rem(lax.iota(jnp.int32, flat), rank)[None, :]
    )
    spread = jnp.where(same_rank, spread, jnp.zeros_like(spread))
    down_map_gradient = dot(spread, down_parts, 0, 1).reshape(slots, rank, down_columns)
    up_map_gradient = dot(spread, up_parts, 0, 1).reshape(slots, rank, up_columns)

    input_gradient = input_gradients(output_gradient, weight, lora_grad, down)
    return (input_gradient, down_map_gradient, up_map_gradient)


def solution(mesh):
    return jax.shard_map(
        functools.partial(shards, mesh.shape["dp"]),
        mesh=mesh,
        in_specs=(
            P(("group", "dp", "adapter"), None),
            P(("group", "dp", "adapter"), None),
            P("dp", None),
            P("group", None, ("dp", "adapter")),
            P("group", None, ("dp", "adapter")),
            P(("group", "dp", "adapter"), None),
            P(("group", "dp", "adapter"), None),
            P("group"),
        ),
        out_specs=(
            P(("group", "dp", "adapter"), None),
            P("group", None, ("dp", "adapter")),
            P("group", None, ("dp", "adapter")),
        ),
        check_vma=False,
    )
```

```python
import functools

import jax
import jax.numpy as jnp
from jax import lax
from jax.experimental import pallas as pl
from jax.experimental.pallas import tpu as pltpu
from jax.sharding import PartitionSpec as P

adapter_scale = 2.0
MESH = pl.DeviceIdType.MESH


def ring_position(d, n):
    odd = lax.rem(d, 2)
    half = lax.div(d, 2)
    return (1 - odd) * half + odd * (n - 1 - half)


def ring_device(p, n):
    p = lax.rem(p + n, n)
    upper = lax.div(p, n // 2)
    return (1 - upper) * (2 * p) + upper * (2 * (n - 1 - p) + 1)


class Ring:
    def __init__(self, n, items, sems):
        self.n, self.items = n, items
        self.ring_send, self.ring_recv, self.side_send, self.side_recv, self.local = sems[:5]
        self.pair_sems = sems[5:]
        self.me = lax.axis_index("dp")
        self.group = lax.axis_index("group")
        self.half = lax.rem(self.group, 2)
        self.pairs = {}
        self.lane = lax.axis_index("adapter")
        self.pos = ring_position(self.me, n)
        self.right = ring_device(self.pos + 1, n)
        self.left = ring_device(self.pos + n - 1, n)
        self.steps = n // 2
        self.copies = {}
        self.sides = []
        self.locals = []

    def window(self, item, device, step, way):
        rows = item[2]
        if step < self.steps - 1:
            return 0, rows
        if rows % 32 == 0:
            return (0, rows // 2) if way == 0 else (rows // 2, rows // 2)
        return (0, rows) if way == 0 else (0, 0)

    def target_rows(self, item, device, lane, start, count, half=None):
        rows = item[2]
        if item[3]:
            half = self.half if half is None else half
            block = device * 4 + half * 2 + lane
        else:
            block = device * 2 + lane
        return item[1].at[pl.ds(pl.multiple_of(block * rows + start, 16), count)]

    def begin(self):
        for i in range(len(self.items)):
            self.send(i, 0)
        for i, item in enumerate(self.items):
            if not item[3]:
                self.side(i, item[0], self.me, 0, item[2], 0)
        for i, (source, target, rows, shared) in enumerate(self.items):
            cuts = 4 if shared else 1
            for cut in range(cuts):
                block = self.me * 4 + cut if shared else self.me * 2 + self.lane
                own = pltpu.make_async_copy(
                    source.at[pl.ds(cut * rows, rows)],
                    target.at[pl.ds(pl.multiple_of(block * rows, 16), rows)],
                    self.local.at[i, cut],
                )
                own.start()
                self.locals.append(own)

    def send(self, i, step):
        item = self.items[i]
        for way in (0, 1):
            start, count = self.window(item, None, step, way)
            if count == 0:
                continue
            back = self.n - step if way == 0 else step
            device = ring_device(self.pos + back, self.n)
            target = self.target_rows(item, device, self.lane, start, count)
            if step == 0:
                base = start
                if item[3]:
                    base = pl.multiple_of((self.half * 2 + self.lane) * item[2] + start, 16)
                source = item[0].at[pl.ds(base, count)]
            else:
                source = target
            copy = pltpu.make_async_remote_copy(
                src_ref=source,
                dst_ref=target,
                send_sem=self.ring_send.at[i, way, step],
                recv_sem=self.ring_recv.at[i, way, step],
                device_id={"dp": self.right if way == 0 else self.left},
                device_id_type=MESH,
            )
            copy.start()
            self.copies[i, way, step] = copy

    def pair(self, i, block, slot):
        copy = pltpu.make_async_remote_copy(
            src_ref=block,
            dst_ref=block,
            send_sem=self.pair_sems[0].at[i, slot],
            recv_sem=self.pair_sems[1].at[i, slot],
            device_id={"group": self.group + 1 - 2 * self.half},
            device_id_type=MESH,
        )
        copy.start()
        self.pairs[i, slot] = copy

    def side(self, i, source, device, start, count, slot, half=None):
        item = self.items[i]
        copy = pltpu.make_async_remote_copy(
            src_ref=source,
            dst_ref=self.target_rows(item, device, self.lane, start, count, half),
            send_sem=self.side_send.at[i, slot],
            recv_sem=self.side_recv.at[i, slot],
            device_id={"adapter": 1 - self.lane},
            device_id_type=MESH,
        )
        copy.start()
        self.sides.append(copy)

    def arrived(self, step):
        for i, item in enumerate(self.items):
            for way in (0, 1):
                start, count = self.window(item, None, step, way)
                if count:
                    ahead = self.n - 1 - step if way == 0 else 1 + step
                    yield i, 1 + 2 * step + way, ring_device(self.pos + ahead, self.n), start, count

    def run(self):
        for step in range(self.steps):
            for i, item in enumerate(self.items):
                for way in (0, 1):
                    if (i, way, step) in self.copies:
                        self.copies[i, way, step].wait_recv()
                if step + 1 < self.steps:
                    self.send(i, step + 1)
            for i, slot, device, start, count in self.arrived(step):
                item = self.items[i]
                block = self.target_rows(item, device, self.lane, start, count)
                if item[3]:
                    self.pair(i, block, slot)
                self.side(i, block, device, start, count, slot)
            if step:
                self.cross(step - 1)
        self.cross(self.steps - 1)

    def cross(self, step):
        for i, slot, device, start, count in self.arrived(step):
            item = self.items[i]
            if item[3]:
                self.pairs[i, slot].wait_recv()
                block = self.target_rows(item, device, self.lane, start, count, 1 - self.half)
                self.side(i, block, device, start, count, self.n + slot, 1 - self.half)

    def finish(self):
        for copy in self.copies.values():
            copy.wait_send()
        for copy in self.pairs.values():
            copy.wait_send()
        for copy in self.sides:
            copy.wait()
        for copy in self.locals:
            copy.wait()


def ring_scratch(n, items):
    return [
        pltpu.SemaphoreType.DMA((items, 2, n // 2)),
        pltpu.SemaphoreType.DMA((items, 2, n // 2)),
        pltpu.SemaphoreType.DMA((items, 1 + 2 * n)),
        pltpu.SemaphoreType.DMA((items, 1 + 2 * n)),
        pltpu.SemaphoreType.DMA((items, 4)),
    ] + [pltpu.SemaphoreType.DMA((items, 1 + n))] * 2


def greet_ring(barrier, n):
    lane, pos = lax.axis_index("adapter"), ring_position(lax.axis_index("dp"), n)
    for device in (ring_device(pos + 1, n), ring_device(pos + n - 1, n)):
        pl.semaphore_signal(barrier, inc=1, device_id={"dp": device}, device_id_type=MESH)
    pl.semaphore_signal(barrier, inc=1, device_id={"adapter": 1 - lane}, device_id_type=MESH)
    group = lax.axis_index("group")
    other = group + 1 - 2 * lax.rem(group, 2)
    pl.semaphore_signal(barrier, inc=1, device_id={"group": other}, device_id_type=MESH)
    pl.semaphore_wait(barrier, 4)


def gather_kernel(n, weight_ref, down_ref, up_ref, weight_out, down_out, up_out, *sems):
    greet_ring(pltpu.get_barrier_semaphore(), n)
    items = [
        (weight_ref, weight_out, weight_ref.shape[0] // 4, True),
        (down_ref, down_out, down_ref.shape[0], False),
        (up_ref, up_out, up_ref.shape[0], False),
    ]
    ring = Ring(n, items, sems)
    ring.begin()
    ring.run()
    ring.finish()


def exchange_kernel(n, down_ref, up_ref, hot_ref, down_out, up_out, hot_out, send_sem, recv_sem, local_sem):
    devices = 2 * n
    me = lax.axis_index("dp") * 2 + lax.axis_index("adapter")
    barrier = pltpu.get_barrier_semaphore()

    def peer_of(k):
        peer = lax.rem(me + k, devices)
        return {"dp": lax.div(peer, 2), "adapter": lax.rem(peer, 2)}, peer

    def greet(k, carry):
        pl.semaphore_signal(barrier, inc=1, device_id=peer_of(k)[0], device_id_type=MESH)
        return carry

    lax.fori_loop(1, devices, greet, 0)
    pl.semaphore_wait(barrier, devices - 1)

    rows_down, rows_up = down_out.shape[0], up_out.shape[0]
    wide = down_ref.shape[1]

    def parts(owner, sender):
        place = pl.ds(pl.multiple_of(sender * wide, 128), wide)
        return (
            (down_ref.at[pl.ds(pl.multiple_of(owner * rows_down, 16), rows_down)], down_out.at[:, place]),
            (up_ref.at[pl.ds(pl.multiple_of(owner * rows_up, 16), rows_up)], up_out.at[:, place]),
            (hot_ref, hot_out.at[sender]),
        )

    def copies(k):
        device, peer = peer_of(k)
        return [
            pltpu.make_async_remote_copy(
                src_ref=source,
                dst_ref=target,
                send_sem=send_sem.at[i, k],
                recv_sem=recv_sem.at[i, k],
                device_id=device,
                device_id_type=MESH,
            )
            for i, (source, target) in enumerate(parts(peer, me))
        ]

    def start(k, carry):
        for copy in copies(k):
            copy.start()
        return carry

    own = [
        pltpu.make_async_copy(source, target, local_sem.at[i]) for i, (source, target) in enumerate(parts(me, me))
    ]
    lax.fori_loop(1, devices, start, 0)
    for copy in own:
        copy.start()

    def end(k, carry):
        for copy in copies(k):
            copy.wait()
        return carry

    lax.fori_loop(1, devices, end, 0)
    for copy in own:
        copy.wait()


def call(kernel, outs, operands, scratch, collective_id):
    anywhere = pl.BlockSpec(memory_space=pl.ANY)
    return pl.pallas_call(
        kernel,
        out_shape=outs,
        in_specs=[anywhere] * len(operands),
        out_specs=[anywhere] * len(outs),
        scratch_shapes=scratch,
        compiler_params=pltpu.CompilerParams(collective_id=collective_id, has_side_effects=True),
    )(*operands)


def input_gradient_kernel(grad_ref, weight_ref, lora_ref, down_ref, out_ref):
    total = dot(grad_ref[...], weight_ref[...], 1, 1) + dot(lora_ref[...], down_ref[...], 1, 1)
    out_ref[...] = total.astype(out_ref.dtype)


def input_gradients(output_gradient, weight, lora_grad, down):
    tok, outputs = output_gradient.shape
    width, flat = down.shape
    columns = 512
    return pl.pallas_call(
        input_gradient_kernel,
        grid=(width // columns,),
        out_shape=jax.ShapeDtypeStruct((tok, width), output_gradient.dtype),
        in_specs=[
            pl.BlockSpec((tok, outputs), lambda i: (0, 0)),
            pl.BlockSpec((columns, outputs), lambda i: (i, 0)),
            pl.BlockSpec((tok, flat), lambda i: (0, 0)),
            pl.BlockSpec((columns, flat), lambda i: (i, 0)),
        ],
        out_specs=pl.BlockSpec((tok, columns), lambda i: (0, i)),
        compiler_params=pltpu.CompilerParams(vmem_limit_bytes=32 * 1024 * 1024),
        cost_estimate=pl.CostEstimate(
            flops=2 * tok * width * (outputs + flat),
            bytes_accessed=2 * (width * (outputs + flat) + tok * (outputs + flat + width)),
            transcendentals=0,
        ),
    )(output_gradient, weight, lora_grad, down)


def token_slots(segment_length_quota, segment_tenant_id, tenant_adapter_slot, tok):
    ends = jnp.cumsum(segment_length_quota[0])
    starts = ends - segment_length_quota[0]
    position = lax.iota(jnp.int32, tok)[:, None]
    seg_hot = (position >= starts[None, :]) & (position < ends[None, :])
    count = tenant_adapter_slot.shape[0]
    tenant_hot = segment_tenant_id[0][:, None] == lax.iota(jnp.int32, count)[None, :]
    slot = jnp.sum(tenant_hot.astype(jnp.int32) * tenant_adapter_slot[None, :], axis=1)
    return seg_hot, slot


def dot(left, right, left_dim, right_dim):
    return lax.dot_general(
        left, right, (((left_dim,), (right_dim,)), ((), ())), preferred_element_type=jnp.float32
    )


def shards(
    n,
    hidden_input,
    output_gradient,
    frozen_value_weight,
    adapter_down_maps,
    adapter_up_maps,
    segment_length_quota,
    segment_tenant_id,
    tenant_adapter_slot,
):
    tok, width = hidden_input.shape
    outputs = output_gradient.shape[1]
    slots, rank, down_columns = adapter_down_maps.shape
    up_columns = adapter_up_maps.shape[2]
    segs = segment_length_quota.shape[1]
    flat, wide, devices = slots * rank, segs * rank, 2 * n
    bf16 = jnp.bfloat16

    down_own = adapter_down_maps.reshape(flat, down_columns).T
    up_own = adapter_up_maps.reshape(flat, up_columns).T
    weight, down, up = call(
        functools.partial(gather_kernel, n),
        [
            jax.ShapeDtypeStruct((width, outputs), bf16),
            jax.ShapeDtypeStruct((width, flat), bf16),
            jax.ShapeDtypeStruct((outputs, flat), bf16),
        ],
        [frozen_value_weight, down_own, up_own],
        ring_scratch(n, 3),
        0,
    )

    seg_hot, slot = token_slots(segment_length_quota, segment_tenant_id, tenant_adapter_slot, tok)
    slot_hot = slot[:, None] == lax.iota(jnp.int32, slots)[None, :]
    seg_mask = jnp.repeat(seg_hot.astype(jnp.float32), rank, axis=1)
    token_hot = dot(seg_hot.astype(bf16), slot_hot.astype(bf16), 1, 0)
    mask = jnp.repeat(token_hot, rank, axis=1)
    fold = (
        lax.rem(lax.iota(jnp.int32, flat), rank)[:, None] == lax.rem(lax.iota(jnp.int32, wide), rank)[None, :]
    ).astype(bf16)

    lora_in = (dot(hidden_input, down, 1, 0) * mask).astype(bf16)
    lora_grad = (adapter_scale * dot(output_gradient, up, 1, 0) * mask).astype(bf16)
    lora_in_seg = (dot(lora_in, fold, 1, 0) * seg_mask).astype(bf16)
    lora_grad_seg = (dot(lora_grad, fold, 1, 0) * seg_mask).astype(bf16)
    down_term = dot(hidden_input, lora_grad_seg, 0, 0).astype(bf16)
    up_term = (adapter_scale * dot(output_gradient, lora_in_seg, 0, 0)).astype(bf16)

    hot = jnp.pad(slot_hot.astype(bf16), ((0, 16 - segs % 16), (0, 128 - slots % 128)))
    down_parts, up_parts, hots = call(
        functools.partial(exchange_kernel, n),
        [
            jax.ShapeDtypeStruct((down_columns, devices * wide), bf16),
            jax.ShapeDtypeStruct((up_columns, devices * wide), bf16),
            jax.ShapeDtypeStruct((devices,) + hot.shape, bf16),
        ],
        [down_term, up_term, hot],
        [pltpu.SemaphoreType.DMA((3, devices)), pltpu.SemaphoreType.DMA((3, devices)), pltpu.SemaphoreType.DMA((3,))],
        1,
    )

    spread = jnp.repeat(jnp.repeat(hots[:, :segs, :slots].reshape(devices * segs, slots), rank, axis=0), rank, axis=1)
    same_rank = (
        lax.rem(lax.iota(jnp.int32, devices * wide), rank)[:, None]
        == lax.rem(lax.iota(jnp.int32, flat), rank)[None, :]
    )
    spread = jnp.where(same_rank, spread, jnp.zeros_like(spread))
    down_map_gradient = dot(spread, down_parts, 0, 1).reshape(slots, rank, down_columns)
    up_map_gradient = dot(spread, up_parts, 0, 1).reshape(slots, rank, up_columns)

    input_gradient = input_gradients(output_gradient, weight, lora_grad, down)
    return (input_gradient, down_map_gradient, up_map_gradient)


def solution(mesh):
    return jax.shard_map(
        functools.partial(shards, mesh.shape["dp"]),
        mesh=mesh,
        in_specs=(
            P(("group", "dp", "adapter"), None),
            P(("group", "dp", "adapter"), None),
            P("dp", None),
            P("group", None, ("dp", "adapter")),
            P("group", None, ("dp", "adapter")),
            P(("group", "dp", "adapter"), None),
            P(("group", "dp", "adapter"), None),
            P("group"),
        ),
        out_specs=(
            P(("group", "dp", "adapter"), None),
            P("group", None, ("dp", "adapter")),
            P("group", None, ("dp", "adapter")),
        ),
        check_vma=False,
    )
```

```python
import functools

import jax
import jax.numpy as jnp
from jax import lax
from jax.experimental import pallas as pl
from jax.experimental.pallas import tpu as pltpu
from jax.sharding import PartitionSpec as P

adapter_scale = 2.0
MESH = pl.DeviceIdType.MESH


def ring_position(d, n):
    odd = lax.rem(d, 2)
    half = lax.div(d, 2)
    return (1 - odd) * half + odd * (n - 1 - half)


def ring_device(p, n):
    p = lax.rem(p + n, n)
    upper = lax.div(p, n // 2)
    return (1 - upper) * (2 * p) + upper * (2 * (n - 1 - p) + 1)


class Ring:
    def __init__(self, n, items, sems):
        self.n, self.items = n, items
        self.ring_send, self.ring_recv, self.side_send, self.side_recv, self.local = sems[:5]
        self.pair_sems = sems[5:]
        self.me = lax.axis_index("dp")
        self.group = lax.axis_index("group")
        self.half = lax.rem(self.group, 2)
        self.pairs = {}
        self.lane = lax.axis_index("adapter")
        self.pos = ring_position(self.me, n)
        self.right = ring_device(self.pos + 1, n)
        self.left = ring_device(self.pos + n - 1, n)
        self.steps = n // 2
        self.copies = {}
        self.sides = []
        self.locals = []

    def window(self, item, device, step, way):
        rows = item[2]
        if step < self.steps - 1:
            return 0, rows
        if rows % 32 == 0:
            return (0, rows // 2) if way == 0 else (rows // 2, rows // 2)
        return (0, rows) if way == 0 else (0, 0)

    def target_rows(self, item, device, lane, start, count, half=None):
        rows = item[2]
        if item[3]:
            half = self.half if half is None else half
            block = device * 4 + half * 2 + lane
        else:
            block = device * 2 + lane
        return item[1].at[pl.ds(pl.multiple_of(block * rows + start, 16), count)]

    def begin(self):
        for i in range(len(self.items)):
            self.send(i, 0)
        for i, item in enumerate(self.items):
            if not item[3]:
                self.side(i, item[0], self.me, 0, item[2], 0)
        for i, (source, target, rows, shared) in enumerate(self.items):
            cuts = 4 if shared else 1
            for cut in range(cuts):
                block = self.me * 4 + cut if shared else self.me * 2 + self.lane
                own = pltpu.make_async_copy(
                    source.at[pl.ds(cut * rows, rows)],
                    target.at[pl.ds(pl.multiple_of(block * rows, 16), rows)],
                    self.local.at[i, cut],
                )
                own.start()
                self.locals.append(own)

    def send(self, i, step):
        item = self.items[i]
        for way in (0, 1):
            start, count = self.window(item, None, step, way)
            if count == 0:
                continue
            back = self.n - step if way == 0 else step
            device = ring_device(self.pos + back, self.n)
            target = self.target_rows(item, device, self.lane, start, count)
            if step == 0:
                base = start
                if item[3]:
                    base = pl.multiple_of((self.half * 2 + self.lane) * item[2] + start, 16)
                source = item[0].at[pl.ds(base, count)]
            else:
                source = target
            copy = pltpu.make_async_remote_copy(
                src_ref=source,
                dst_ref=target,
                send_sem=self.ring_send.at[i, way, step],
                recv_sem=self.ring_recv.at[i, way, step],
                device_id={"dp": self.right if way == 0 else self.left},
                device_id_type=MESH,
            )
            copy.start()
            self.copies[i, way, step] = copy

    def pair(self, i, block, slot):
        copy = pltpu.make_async_remote_copy(
            src_ref=block,
            dst_ref=block,
            send_sem=self.pair_sems[0].at[i, slot],
            recv_sem=self.pair_sems[1].at[i, slot],
            device_id={"group": self.group + 1 - 2 * self.half},
            device_id_type=MESH,
        )
        copy.start()
        self.pairs[i, slot] = copy

    def side(self, i, source, device, start, count, slot, half=None):
        item = self.items[i]
        copy = pltpu.make_async_remote_copy(
            src_ref=source,
            dst_ref=self.target_rows(item, device, self.lane, start, count, half),
            send_sem=self.side_send.at[i, slot],
            recv_sem=self.side_recv.at[i, slot],
            device_id={"adapter": 1 - self.lane},
            device_id_type=MESH,
        )
        copy.start()
        self.sides.append(copy)

    def arrived(self, step):
        for i, item in enumerate(self.items):
            for way in (0, 1):
                start, count = self.window(item, None, step, way)
                if count:
                    ahead = self.n - 1 - step if way == 0 else 1 + step
                    yield i, 1 + 2 * step + way, ring_device(self.pos + ahead, self.n), start, count

    def run(self):
        for step in range(self.steps):
            for i, item in enumerate(self.items):
                for way in (0, 1):
                    if (i, way, step) in self.copies:
                        self.copies[i, way, step].wait_recv()
                if step + 1 < self.steps:
                    self.send(i, step + 1)
            for i, slot, device, start, count in self.arrived(step):
                item = self.items[i]
                block = self.target_rows(item, device, self.lane, start, count)
                if item[3]:
                    self.pair(i, block, slot)
                self.side(i, block, device, start, count, slot)
            if step:
                self.cross(step - 1)
        self.cross(self.steps - 1)

    def cross(self, step):
        for i, slot, device, start, count in self.arrived(step):
            item = self.items[i]
            if item[3]:
                self.pairs[i, slot].wait_recv()
                block = self.target_rows(item, device, self.lane, start, count, 1 - self.half)
                self.side(i, block, device, start, count, self.n + slot, 1 - self.half)

    def finish(self):
        for copy in self.copies.values():
            copy.wait_send()
        for copy in self.pairs.values():
            copy.wait_send()
        for copy in self.sides:
            copy.wait()
        for copy in self.locals:
            copy.wait()


def ring_scratch(n, items):
    return [
        pltpu.SemaphoreType.DMA((items, 2, n // 2)),
        pltpu.SemaphoreType.DMA((items, 2, n // 2)),
        pltpu.SemaphoreType.DMA((items, 1 + 2 * n)),
        pltpu.SemaphoreType.DMA((items, 1 + 2 * n)),
        pltpu.SemaphoreType.DMA((items, 4)),
    ] + [pltpu.SemaphoreType.DMA((items, 1 + n))] * 2


def greet_ring(barrier, n):
    lane, pos = lax.axis_index("adapter"), ring_position(lax.axis_index("dp"), n)
    for device in (ring_device(pos + 1, n), ring_device(pos + n - 1, n)):
        pl.semaphore_signal(barrier, inc=1, device_id={"dp": device}, device_id_type=MESH)
    pl.semaphore_signal(barrier, inc=1, device_id={"adapter": 1 - lane}, device_id_type=MESH)
    group = lax.axis_index("group")
    other = group + 1 - 2 * lax.rem(group, 2)
    pl.semaphore_signal(barrier, inc=1, device_id={"group": other}, device_id_type=MESH)
    pl.semaphore_wait(barrier, 4)


def gather_kernel(n, weight_ref, down_ref, up_ref, weight_out, down_out, up_out, *sems):
    greet_ring(pltpu.get_barrier_semaphore(), n)
    items = [
        (weight_ref, weight_out, weight_ref.shape[0] // 4, True),
        (down_ref, down_out, down_ref.shape[0], False),
        (up_ref, up_out, up_ref.shape[0], False),
    ]
    ring = Ring(n, items, sems)
    ring.begin()
    ring.run()
    ring.finish()


def exchange_kernel(n, down_ref, up_ref, hot_ref, grad_ref, weight_ref, lora_ref, maps_ref, *rest):
    down_out, up_out, hot_out, input_out, send_sem, recv_sem, local_sem = rest
    devices = 2 * n
    me = lax.axis_index("dp") * 2 + lax.axis_index("adapter")
    barrier = pltpu.get_barrier_semaphore()

    def peer_of(k):
        peer = lax.rem(me + k, devices)
        return {"dp": lax.div(peer, 2), "adapter": lax.rem(peer, 2)}, peer

    def greet(k, carry):
        pl.semaphore_signal(barrier, inc=1, device_id=peer_of(k)[0], device_id_type=MESH)
        return carry

    lax.fori_loop(1, devices, greet, 0)
    pl.semaphore_wait(barrier, devices - 1)

    rows_down, rows_up = down_out.shape[0], up_out.shape[0]
    wide = down_ref.shape[1]

    def parts(owner, sender):
        place = pl.ds(pl.multiple_of(sender * wide, 128), wide)
        return (
            (down_ref.at[pl.ds(pl.multiple_of(owner * rows_down, 16), rows_down)], down_out.at[:, place]),
            (up_ref.at[pl.ds(pl.multiple_of(owner * rows_up, 16), rows_up)], up_out.at[:, place]),
            (hot_ref, hot_out.at[sender]),
        )

    def copies(k):
        device, peer = peer_of(k)
        return [
            pltpu.make_async_remote_copy(
                src_ref=source,
                dst_ref=target,
                send_sem=send_sem.at[i, k],
                recv_sem=recv_sem.at[i, k],
                device_id=device,
                device_id_type=MESH,
            )
            for i, (source, target) in enumerate(parts(peer, me))
        ]

    def start(k, carry):
        for copy in copies(k):
            copy.start()
        return carry

    own = [
        pltpu.make_async_copy(source, target, local_sem.at[i]) for i, (source, target) in enumerate(parts(me, me))
    ]
    lax.fori_loop(1, devices, start, 0)
    for copy in own:
        copy.start()
    input_gradient_pipeline((grad_ref, weight_ref, lora_ref, maps_ref), input_out)

    def end(k, carry):
        for copy in copies(k):
            copy.wait()
        return carry

    lax.fori_loop(1, devices, end, 0)
    for copy in own:
        copy.wait()


def call(kernel, outs, operands, scratch, collective_id):
    anywhere = pl.BlockSpec(memory_space=pl.ANY)
    return pl.pallas_call(
        kernel,
        out_shape=outs,
        in_specs=[anywhere] * len(operands),
        out_specs=[anywhere] * len(outs),
        scratch_shapes=scratch,
        compiler_params=pltpu.CompilerParams(
            collective_id=collective_id, has_side_effects=True, vmem_limit_bytes=32 * 1024 * 1024
        ),
    )(*operands)


def input_gradient_kernel(grad_ref, weight_ref, lora_ref, down_ref, out_ref):
    total = dot(grad_ref[...], weight_ref[...], 1, 1) + dot(lora_ref[...], down_ref[...], 1, 1)
    out_ref[...] = total.astype(out_ref.dtype)


def input_gradient_pipeline(operands, out):
    output_gradient, weight, lora_grad, down = operands
    tok, outputs = output_gradient.shape
    width, flat = down.shape
    columns = 512
    pltpu.emit_pipeline(
        input_gradient_kernel,
        grid=(width // columns,),
        in_specs=[
            pl.BlockSpec((tok, outputs), lambda i: (0, 0)),
            pl.BlockSpec((columns, outputs), lambda i: (i, 0)),
            pl.BlockSpec((tok, flat), lambda i: (0, 0)),
            pl.BlockSpec((columns, flat), lambda i: (i, 0)),
        ],
        out_specs=[pl.BlockSpec((tok, columns), lambda i: (0, i))],
    )(output_gradient, weight, lora_grad, down, out)


def token_slots(segment_length_quota, segment_tenant_id, tenant_adapter_slot, tok):
    ends = jnp.cumsum(segment_length_quota[0])
    starts = ends - segment_length_quota[0]
    position = lax.iota(jnp.int32, tok)[:, None]
    seg_hot = (position >= starts[None, :]) & (position < ends[None, :])
    count = tenant_adapter_slot.shape[0]
    tenant_hot = segment_tenant_id[0][:, None] == lax.iota(jnp.int32, count)[None, :]
    slot = jnp.sum(tenant_hot.astype(jnp.int32) * tenant_adapter_slot[None, :], axis=1)
    return seg_hot, slot


def dot(left, right, left_dim, right_dim):
    return lax.dot_general(
        left, right, (((left_dim,), (right_dim,)), ((), ())), preferred_element_type=jnp.float32
    )


def shards(
    n,
    hidden_input,
    output_gradient,
    frozen_value_weight,
    adapter_down_maps,
    adapter_up_maps,
    segment_length_quota,
    segment_tenant_id,
    tenant_adapter_slot,
):
    tok, width = hidden_input.shape
    outputs = output_gradient.shape[1]
    slots, rank, down_columns = adapter_down_maps.shape
    up_columns = adapter_up_maps.shape[2]
    segs = segment_length_quota.shape[1]
    flat, wide, devices = slots * rank, segs * rank, 2 * n
    bf16 = jnp.bfloat16

    down_own = adapter_down_maps.reshape(flat, down_columns).T
    up_own = adapter_up_maps.reshape(flat, up_columns).T
    weight, down, up = call(
        functools.partial(gather_kernel, n),
        [
            jax.ShapeDtypeStruct((width, outputs), bf16),
            jax.ShapeDtypeStruct((width, flat), bf16),
            jax.ShapeDtypeStruct((outputs, flat), bf16),
        ],
        [frozen_value_weight, down_own, up_own],
        ring_scratch(n, 3),
        0,
    )

    seg_hot, slot = token_slots(segment_length_quota, segment_tenant_id, tenant_adapter_slot, tok)
    slot_hot = slot[:, None] == lax.iota(jnp.int32, slots)[None, :]
    seg_mask = jnp.repeat(seg_hot.astype(jnp.float32), rank, axis=1)
    token_hot = dot(seg_hot.astype(bf16), slot_hot.astype(bf16), 1, 0)
    mask = jnp.repeat(token_hot, rank, axis=1)
    fold = (
        lax.rem(lax.iota(jnp.int32, flat), rank)[:, None] == lax.rem(lax.iota(jnp.int32, wide), rank)[None, :]
    ).astype(bf16)

    lora_in = (dot(hidden_input, down, 1, 0) * mask).astype(bf16)
    lora_grad = (adapter_scale * dot(output_gradient, up, 1, 0) * mask).astype(bf16)
    lora_in_seg = (dot(lora_in, fold, 1, 0) * seg_mask).astype(bf16)
    lora_grad_seg = (dot(lora_grad, fold, 1, 0) * seg_mask).astype(bf16)
    down_term = dot(hidden_input, lora_grad_seg, 0, 0).astype(bf16)
    up_term = (adapter_scale * dot(output_gradient, lora_in_seg, 0, 0)).astype(bf16)

    hot = jnp.pad(slot_hot.astype(bf16), ((0, 16 - segs % 16), (0, 128 - slots % 128)))
    down_parts, up_parts, hots, input_gradient = call(
        functools.partial(exchange_kernel, n),
        [
            jax.ShapeDtypeStruct((down_columns, devices * wide), bf16),
            jax.ShapeDtypeStruct((up_columns, devices * wide), bf16),
            jax.ShapeDtypeStruct((devices,) + hot.shape, bf16),
            jax.ShapeDtypeStruct((tok, width), bf16),
        ],
        [down_term, up_term, hot, output_gradient, weight, lora_grad, down],
        [pltpu.SemaphoreType.DMA((3, devices)), pltpu.SemaphoreType.DMA((3, devices)), pltpu.SemaphoreType.DMA((3,))],
        1,
    )

    spread = jnp.repeat(jnp.repeat(hots[:, :segs, :slots].reshape(devices * segs, slots), rank, axis=0), rank, axis=1)
    same_rank = (
        lax.rem(lax.iota(jnp.int32, devices * wide), rank)[:, None]
        == lax.rem(lax.iota(jnp.int32, flat), rank)[None, :]
    )
    spread = jnp.where(same_rank, spread, jnp.zeros_like(spread))
    down_map_gradient = dot(spread, down_parts, 0, 1).reshape(slots, rank, down_columns)
    up_map_gradient = dot(spread, up_parts, 0, 1).reshape(slots, rank, up_columns)

    return (input_gradient, down_map_gradient, up_map_gradient)


def solution(mesh):
    return jax.shard_map(
        functools.partial(shards, mesh.shape["dp"]),
        mesh=mesh,
        in_specs=(
            P(("group", "dp", "adapter"), None),
            P(("group", "dp", "adapter"), None),
            P("dp", None),
            P("group", None, ("dp", "adapter")),
            P("group", None, ("dp", "adapter")),
            P(("group", "dp", "adapter"), None),
            P(("group", "dp", "adapter"), None),
            P("group"),
        ),
        out_specs=(
            P(("group", "dp", "adapter"), None),
            P("group", None, ("dp", "adapter")),
            P("group", None, ("dp", "adapter")),
        ),
        check_vma=False,
    )
```

```python
import functools

import jax
import jax.numpy as jnp
from jax import lax
from jax.experimental import pallas as pl
from jax.experimental.pallas import tpu as pltpu
from jax.sharding import PartitionSpec as P

adapter_scale = 2.0
MESH = pl.DeviceIdType.MESH


def ring_position(d, n):
    odd = lax.rem(d, 2)
    half = lax.div(d, 2)
    return (1 - odd) * half + odd * (n - 1 - half)


def ring_device(p, n):
    p = lax.rem(p + n, n)
    upper = lax.div(p, n // 2)
    return (1 - upper) * (2 * p) + upper * (2 * (n - 1 - p) + 1)


class Ring:
    def __init__(self, n, items, sems):
        self.n, self.items = n, items
        self.ring_send, self.ring_recv, self.side_send, self.side_recv, self.local = sems[:5]
        self.pair_sems = sems[5:]
        self.me = lax.axis_index("dp")
        self.group = lax.axis_index("group")
        self.half = lax.rem(self.group, 2)
        self.pairs = {}
        self.lane = lax.axis_index("adapter")
        self.pos = ring_position(self.me, n)
        self.right = ring_device(self.pos + 1, n)
        self.left = ring_device(self.pos + n - 1, n)
        self.steps = n // 2
        self.copies = {}
        self.sides = []
        self.locals = []

    def window(self, item, device, step, way):
        rows = item[2]
        if step < self.steps - 1:
            return 0, rows
        if rows % 32 == 0:
            return (0, rows // 2) if way == 0 else (rows // 2, rows // 2)
        return (0, rows) if way == 0 else (0, 0)

    def target_rows(self, item, device, lane, start, count, half=None):
        rows = item[2]
        if item[3]:
            half = self.half if half is None else half
            block = device * 4 + half * 2 + lane
        else:
            block = device * 2 + lane
        return item[1].at[pl.ds(pl.multiple_of(block * rows + start, 16), count)]

    def begin(self):
        for i in range(len(self.items)):
            self.send(i, 0)
        for i, item in enumerate(self.items):
            if not item[3]:
                self.side(i, item[0], self.me, 0, item[2], 0)
        for i, (source, target, rows, shared) in enumerate(self.items):
            cuts = 4 if shared else 1
            for cut in range(cuts):
                block = self.me * 4 + cut if shared else self.me * 2 + self.lane
                own = pltpu.make_async_copy(
                    source.at[pl.ds(cut * rows, rows)],
                    target.at[pl.ds(pl.multiple_of(block * rows, 16), rows)],
                    self.local.at[i, cut],
                )
                own.start()
                self.locals.append(own)

    def send(self, i, step):
        item = self.items[i]
        for way in (0, 1):
            start, count = self.window(item, None, step, way)
            if count == 0:
                continue
            back = self.n - step if way == 0 else step
            device = ring_device(self.pos + back, self.n)
            target = self.target_rows(item, device, self.lane, start, count)
            if step == 0:
                base = start
                if item[3]:
                    base = pl.multiple_of((self.half * 2 + self.lane) * item[2] + start, 16)
                source = item[0].at[pl.ds(base, count)]
            else:
                source = target
            copy = pltpu.make_async_remote_copy(
                src_ref=source,
                dst_ref=target,
                send_sem=self.ring_send.at[i, way, step],
                recv_sem=self.ring_recv.at[i, way, step],
                device_id={"dp": self.right if way == 0 else self.left},
                device_id_type=MESH,
            )
            copy.start()
            self.copies[i, way, step] = copy

    def pair(self, i, block, slot):
        copy = pltpu.make_async_remote_copy(
            src_ref=block,
            dst_ref=block,
            send_sem=self.pair_sems[0].at[i, slot],
            recv_sem=self.pair_sems[1].at[i, slot],
            device_id={"group": self.group + 1 - 2 * self.half},
            device_id_type=MESH,
        )
        copy.start()
        self.pairs[i, slot] = copy

    def side(self, i, source, device, start, count, slot, half=None):
        item = self.items[i]
        copy = pltpu.make_async_remote_copy(
            src_ref=source,
            dst_ref=self.target_rows(item, device, self.lane, start, count, half),
            send_sem=self.side_send.at[i, slot],
            recv_sem=self.side_recv.at[i, slot],
            device_id={"adapter": 1 - self.lane},
            device_id_type=MESH,
        )
        copy.start()
        self.sides.append(copy)

    def arrived(self, step):
        for i, item in enumerate(self.items):
            for way in (0, 1):
                start, count = self.window(item, None, step, way)
                if count:
                    ahead = self.n - 1 - step if way == 0 else 1 + step
                    yield i, 1 + 2 * step + way, ring_device(self.pos + ahead, self.n), start, count

    def run(self):
        for step in range(self.steps):
            for i, item in enumerate(self.items):
                for way in (0, 1):
                    if (i, way, step) in self.copies:
                        self.copies[i, way, step].wait_recv()
                if step + 1 < self.steps:
                    self.send(i, step + 1)
                for which, slot, device, start, count in self.arrived(step):
                    if which != i:
                        continue
                    block = self.target_rows(item, device, self.lane, start, count)
                    if item[3]:
                        self.pair(i, block, slot)
                    self.side(i, block, device, start, count, slot)
            if step >= 2:
                self.cross(step - 2)
        for step in range(max(self.steps - 2, 0), self.steps):
            self.cross(step)

    def cross(self, step):
        for i, slot, device, start, count in self.arrived(step):
            item = self.items[i]
            if item[3]:
                self.pairs[i, slot].wait_recv()
                block = self.target_rows(item, device, self.lane, start, count, 1 - self.half)
                self.side(i, block, device, start, count, self.n + slot, 1 - self.half)

    def finish(self):
        for copy in self.copies.values():
            copy.wait_send()
        for copy in self.pairs.values():
            copy.wait_send()
        for copy in self.sides:
            copy.wait()
        for copy in self.locals:
            copy.wait()


def ring_scratch(n, items):
    return [
        pltpu.SemaphoreType.DMA((items, 2, n // 2)),
        pltpu.SemaphoreType.DMA((items, 2, n // 2)),
        pltpu.SemaphoreType.DMA((items, 1 + 2 * n)),
        pltpu.SemaphoreType.DMA((items, 1 + 2 * n)),
        pltpu.SemaphoreType.DMA((items, 4)),
    ] + [pltpu.SemaphoreType.DMA((items, 1 + n))] * 2


def greet_ring(barrier, n):
    lane, pos = lax.axis_index("adapter"), ring_position(lax.axis_index("dp"), n)
    for device in (ring_device(pos + 1, n), ring_device(pos + n - 1, n)):
        pl.semaphore_signal(barrier, inc=1, device_id={"dp": device}, device_id_type=MESH)
    pl.semaphore_signal(barrier, inc=1, device_id={"adapter": 1 - lane}, device_id_type=MESH)
    group = lax.axis_index("group")
    other = group + 1 - 2 * lax.rem(group, 2)
    pl.semaphore_signal(barrier, inc=1, device_id={"group": other}, device_id_type=MESH)
    pl.semaphore_wait(barrier, 4)


def gather_kernel(n, weight_ref, down_ref, up_ref, weight_out, down_out, up_out, *sems):
    greet_ring(pltpu.get_barrier_semaphore(), n)
    items = [
        (weight_ref, weight_out, weight_ref.shape[0] // 4, True),
        (down_ref, down_out, down_ref.shape[0], False),
        (up_ref, up_out, up_ref.shape[0], False),
    ]
    ring = Ring(n, items, sems)
    ring.begin()
    ring.run()
    ring.finish()


def exchange_kernel(n, down_ref, up_ref, hot_ref, grad_ref, weight_ref, lora_ref, maps_ref, *rest):
    down_out, up_out, hot_out, input_out, send_sem, recv_sem, local_sem = rest
    devices = 2 * n
    me = lax.axis_index("dp") * 2 + lax.axis_index("adapter")
    barrier = pltpu.get_barrier_semaphore()

    def peer_of(k):
        peer = lax.rem(me + k, devices)
        return {"dp": lax.div(peer, 2), "adapter": lax.rem(peer, 2)}, peer

    def greet(k, carry):
        pl.semaphore_signal(barrier, inc=1, device_id=peer_of(k)[0], device_id_type=MESH)
        return carry

    lax.fori_loop(1, devices, greet, 0)
    pl.semaphore_wait(barrier, devices - 1)

    rows_down, rows_up = down_out.shape[0], up_out.shape[0]
    wide = down_ref.shape[1]

    def parts(owner, sender):
        place = pl.ds(pl.multiple_of(sender * wide, 128), wide)
        return (
            (down_ref.at[pl.ds(pl.multiple_of(owner * rows_down, 16), rows_down)], down_out.at[:, place]),
            (up_ref.at[pl.ds(pl.multiple_of(owner * rows_up, 16), rows_up)], up_out.at[:, place]),
            (hot_ref, hot_out.at[sender]),
        )

    def copies(k):
        device, peer = peer_of(k)
        return [
            pltpu.make_async_remote_copy(
                src_ref=source,
                dst_ref=target,
                send_sem=send_sem.at[i, k],
                recv_sem=recv_sem.at[i, k],
                device_id=device,
                device_id_type=MESH,
            )
            for i, (source, target) in enumerate(parts(peer, me))
        ]

    def start(k, carry):
        for copy in copies(k):
            copy.start()
        return carry

    own = [
        pltpu.make_async_copy(source, target, local_sem.at[i]) for i, (source, target) in enumerate(parts(me, me))
    ]
    lax.fori_loop(1, devices, start, 0)
    for copy in own:
        copy.start()
    input_gradient_pipeline((grad_ref, weight_ref, lora_ref, maps_ref), input_out)

    def end(k, carry):
        for copy in copies(k):
            copy.wait()
        return carry

    lax.fori_loop(1, devices, end, 0)
    for copy in own:
        copy.wait()


def call(kernel, outs, operands, scratch, collective_id):
    anywhere = pl.BlockSpec(memory_space=pl.ANY)
    return pl.pallas_call(
        kernel,
        out_shape=outs,
        in_specs=[anywhere] * len(operands),
        out_specs=[anywhere] * len(outs),
        scratch_shapes=scratch,
        compiler_params=pltpu.CompilerParams(
            collective_id=collective_id, has_side_effects=True, vmem_limit_bytes=56 * 1024 * 1024
        ),
    )(*operands)


def input_gradient_kernel(grad_ref, weight_ref, lora_ref, down_ref, out_ref):
    total = dot(grad_ref[...], weight_ref[...], 1, 1) + dot(lora_ref[...], down_ref[...], 1, 1)
    out_ref[...] = total.astype(out_ref.dtype)


def input_gradient_pipeline(operands, out):
    output_gradient, weight, lora_grad, down = operands
    tok, outputs = output_gradient.shape
    width, flat = down.shape
    columns = 512
    pltpu.emit_pipeline(
        input_gradient_kernel,
        grid=(width // columns,),
        in_specs=[
            pl.BlockSpec((tok, outputs), lambda i: (0, 0)),
            pl.BlockSpec((columns, outputs), lambda i: (i, 0)),
            pl.BlockSpec((tok, flat), lambda i: (0, 0)),
            pl.BlockSpec((columns, flat), lambda i: (i, 0)),
        ],
        out_specs=[pl.BlockSpec((tok, columns), lambda i: (0, i))],
    )(output_gradient, weight, lora_grad, down, out)


def token_slots(segment_length_quota, segment_tenant_id, tenant_adapter_slot, tok):
    ends = jnp.cumsum(segment_length_quota[0])
    starts = ends - segment_length_quota[0]
    position = lax.iota(jnp.int32, tok)[:, None]
    seg_hot = (position >= starts[None, :]) & (position < ends[None, :])
    count = tenant_adapter_slot.shape[0]
    tenant_hot = segment_tenant_id[0][:, None] == lax.iota(jnp.int32, count)[None, :]
    slot = jnp.sum(tenant_hot.astype(jnp.int32) * tenant_adapter_slot[None, :], axis=1)
    return seg_hot, slot


def dot(left, right, left_dim, right_dim):
    return lax.dot_general(
        left, right, (((left_dim,), (right_dim,)), ((), ())), preferred_element_type=jnp.float32
    )


def shards(
    n,
    hidden_input,
    output_gradient,
    frozen_value_weight,
    adapter_down_maps,
    adapter_up_maps,
    segment_length_quota,
    segment_tenant_id,
    tenant_adapter_slot,
):
    tok, width = hidden_input.shape
    outputs = output_gradient.shape[1]
    slots, rank, down_columns = adapter_down_maps.shape
    up_columns = adapter_up_maps.shape[2]
    segs = segment_length_quota.shape[1]
    flat, wide, devices = slots * rank, segs * rank, 2 * n
    bf16 = jnp.bfloat16

    down_own = adapter_down_maps.reshape(flat, down_columns).T
    up_own = adapter_up_maps.reshape(flat, up_columns).T
    weight, down, up = call(
        functools.partial(gather_kernel, n),
        [
            jax.ShapeDtypeStruct((width, outputs), bf16),
            jax.ShapeDtypeStruct((width, flat), bf16),
            jax.ShapeDtypeStruct((outputs, flat), bf16),
        ],
        [frozen_value_weight, down_own, up_own],
        ring_scratch(n, 3),
        0,
    )

    seg_hot, slot = token_slots(segment_length_quota, segment_tenant_id, tenant_adapter_slot, tok)
    slot_hot = slot[:, None] == lax.iota(jnp.int32, slots)[None, :]
    seg_mask = jnp.repeat(seg_hot.astype(jnp.float32), rank, axis=1)
    token_hot = dot(seg_hot.astype(bf16), slot_hot.astype(bf16), 1, 0)
    mask = jnp.repeat(token_hot, rank, axis=1)
    fold = (
        lax.rem(lax.iota(jnp.int32, flat), rank)[:, None] == lax.rem(lax.iota(jnp.int32, wide), rank)[None, :]
    ).astype(bf16)

    lora_in = (dot(hidden_input, down, 1, 0) * mask).astype(bf16)
    lora_grad = (adapter_scale * dot(output_gradient, up, 1, 0) * mask).astype(bf16)
    lora_in_seg = (dot(lora_in, fold, 1, 0) * seg_mask).astype(bf16)
    lora_grad_seg = (dot(lora_grad, fold, 1, 0) * seg_mask).astype(bf16)
    down_term = dot(hidden_input, lora_grad_seg, 0, 0).astype(bf16)
    up_term = (adapter_scale * dot(output_gradient, lora_in_seg, 0, 0)).astype(bf16)

    hot = jnp.pad(slot_hot.astype(bf16), ((0, 16 - segs % 16), (0, 128 - slots % 128)))
    down_parts, up_parts, hots, input_gradient = call(
        functools.partial(exchange_kernel, n),
        [
            jax.ShapeDtypeStruct((down_columns, devices * wide), bf16),
            jax.ShapeDtypeStruct((up_columns, devices * wide), bf16),
            jax.ShapeDtypeStruct((devices,) + hot.shape, bf16),
            jax.ShapeDtypeStruct((tok, width), bf16),
        ],
        [down_term, up_term, hot, output_gradient, weight, lora_grad, down],
        [pltpu.SemaphoreType.DMA((3, devices)), pltpu.SemaphoreType.DMA((3, devices)), pltpu.SemaphoreType.DMA((3,))],
        1,
    )

    spread = jnp.repeat(jnp.repeat(hots[:, :segs, :slots].reshape(devices * segs, slots), rank, axis=0), rank, axis=1)
    same_rank = (
        lax.rem(lax.iota(jnp.int32, devices * wide), rank)[:, None]
        == lax.rem(lax.iota(jnp.int32, flat), rank)[None, :]
    )
    spread = jnp.where(same_rank, spread, jnp.zeros_like(spread))
    down_map_gradient = dot(spread, down_parts, 0, 1).reshape(slots, rank, down_columns)
    up_map_gradient = dot(spread, up_parts, 0, 1).reshape(slots, rank, up_columns)

    return (input_gradient, down_map_gradient, up_map_gradient)


def solution(mesh):
    return jax.shard_map(
        functools.partial(shards, mesh.shape["dp"]),
        mesh=mesh,
        in_specs=(
            P(("group", "dp", "adapter"), None),
            P(("group", "dp", "adapter"), None),
            P("dp", None),
            P("group", None, ("dp", "adapter")),
            P("group", None, ("dp", "adapter")),
            P(("group", "dp", "adapter"), None),
            P(("group", "dp", "adapter"), None),
            P("group"),
        ),
        out_specs=(
            P(("group", "dp", "adapter"), None),
            P("group", None, ("dp", "adapter")),
            P("group", None, ("dp", "adapter")),
        ),
        check_vma=False,
    )
```
